128 devices in a mesh: plane: 8 (over z, core), dom: 16 (over x, y).
Axes of the slice: x: 4, y: 4, z: 4, core: 2. Of those that a mesh axis runs over, the one named last changes fastest.
Arguments:
- right_side: float32 [8, 32, 64, 640], P('plane', 'dom'), may hold values from -6 to 6
- inverse_diag: bfloat16 [8, 32, 640, 640], P('plane', 'dom'), may hold values from -0.25 to 0.25
- back_blocks: bfloat16 [8, 32, 2, 640, 640], P('plane', 'dom'), may hold values from -0.125 to 0.125
- back_near: int32 [8, 32, 2], P('plane', 'dom'), may hold values from 0 to 5
- fore_blocks: bfloat16 [8, 32, 2, 640, 640], P('plane', 'dom'), may hold values from -0.125 to 0.125
- fore_near: int32 [8, 32, 2], P('plane', 'dom'), may hold values from 0 to 5
- fringe_blocks: bfloat16 [8, 192, 640, 640], P('plane', 'dom'), may hold values from -0.25 to 0.25
- fringe_donor: int32 [8, 192], P('plane', 'dom'), may hold values from 0 to 1
- fringe_dest: int32 [8, 192, 1], P('plane', 'dom'), may hold values from 0 to 15; in each aligned block of 12 rows (0 to 11, 12 to 23, ..., all dimensions but the last counted through in order) at most 2 rows name the same one
- fringe_slot: int32 [8, 192], P('plane', 'dom'), may hold values from 0 to 1
Outputs:
- adjoint_update: bfloat16 [8, 32, 64, 640], P('plane', 'dom')
The draws below stay inside these ranges and needn't reach their ends.
Inputs may be any that keep to these rules, and one draw needn't show every extreme that they name: `fringe_dest`: among the 12 links of one device, at most 2 name the same destination, and in some device exactly 2 do.
All inputs are finite; a program needn't handle non-finite values.
Results may differ from the reference program's by a relative error of at most 0.029.
Values may be sent and summed in bfloat16 or wider, within the bound.
A program may use at most 128 MiB of HBM per device.

```python
import math
import jax
import jax.numpy as jnp
import numpy as np

BLOCK = 640
CLUSTERS = 2
OBJECTIVES = 64
COUPLED = 2
LINKS = 12
CAPACITY = 2
PLANES = 8
PLANE_CLUSTERS = 32
ALL_LINKS = 192
N_DOM = 16


def plant(values, own_key, least, largest):
    extent = values.shape
    place = [jax.random.randint(jax.random.fold_in(own_key, axis), (), 0, extent[axis]) for axis in range(len(extent))]
    values = values.at[tuple(place)].set(least)
    longest = extent.index(max(extent))
    place[longest] = (place[longest] + 1) % extent[longest]
    return values.at[tuple(place)].set(largest)


def levels(rng, dims, split, smallest, top_value):
    def one(position, shards_of):
        draws = jax.random.uniform(jax.random.fold_in(jax.random.fold_in(rng, 6), position), (shards_of,), jnp.float32, smallest / len(split), top_value / len(split))
        return jnp.repeat(jnp.exp(draws), dims[position] // shards_of).reshape((-1,) + (1,) * (len(dims) - position - 1))

    level = one(*split[0])
    for cut in split[1:]:
        level = level * one(*cut)
    return level


def deal_out(stream_key, own, number, rows, amount, top, reach, lean):
    ranking = jax.random.permutation(stream_key, amount)
    heavy_load, usual = shares(amount, rows * top, reach, lean, True), shares(amount, rows * top, reach, lean, False)
    places = jnp.arange(amount)

    def named(tallies, offset_by):
        used = int((tallies > 0).sum())
        fixed = max(1, used // 4)
        shifted = fixed + (places - fixed + offset_by * (used - fixed)) % max(1, amount - fixed)
        return jnp.zeros((amount,), jnp.int32).at[ranking[jnp.where(places < fixed, places, shifted)]].set(jnp.asarray(tallies, jnp.int32))

    tallies = jnp.where(number % 4 == 0, named(heavy_load, number // 4), named(usual, number - number // 4 - 1))
    mixed = jax.random.permutation(jax.random.fold_in(own, 3), amount)
    source_of, taker = mixed[0:amount // 2 * 2:2], mixed[1:amount // 2 * 2:2]
    room = jnp.minimum(tallies[source_of] - 1, reach - tallies[taker]) // 2
    room = jnp.where((source_of == ranking[0]) | (taker == ranking[0]) | (tallies[taker] == 0), 0, jnp.maximum(room, 0))
    shifted = jax.random.randint(jax.random.fold_in(own, 4), (amount // 2,), 0, 1 << 20) % (room + 1)
    tallies = tallies.at[source_of].add(-shifted).at[taker].add(shifted)
    labels = jnp.searchsorted(jnp.cumsum(tallies), jnp.arange(rows * top), side="right").astype(jnp.int32)
    listing = labels.reshape(top, rows).T
    listing = listing[jax.random.permutation(jax.random.fold_in(own, 1), rows)]
    offset_by = jax.random.randint(jax.random.fold_in(own, 2), (rows, 1), 0, top)
    return jnp.take_along_axis(listing, (jnp.arange(top)[None, :] + offset_by) % top, axis=1)


def shares(amount, total, reach, skew, full):
    loads = [(1 << 20) // math.isqrt(rank ** skew) + 1 for rank in range(1, amount + 1)]
    largest = reach if full else min(reach, max(-(-total // amount), total * loads[0] // sum(loads)))
    least = 1 if total - largest >= amount - 1 else 0
    holding, rest = [largest] + [least] * (amount - 1), total - largest - least * (amount - 1)
    while rest > 0:
        candidates = [i for i in range(1, amount) if holding[i] < largest] or [i for i in range(1, amount) if holding[i] < reach]
        pool, left = sum([loads[i] for i in candidates]), rest
        for i in candidates:
            extra = min(reach - holding[i], max(1, left * loads[i] // pool), rest)
            holding[i] = holding[i] + extra
            rest = rest - extra
    return np.array(holding)


def bell_draw(own_key, extent, deviation, bound, cuts=(), held_as=jnp.bfloat16):
    loudness = levels(own_key, extent, cuts, -0.22, 0.18) if cuts else 1.0
    drawn = jax.random.normal(own_key, extent, jnp.float32) * deviation * loudness
    return jnp.minimum(jnp.maximum(drawn, -bound), bound).astype(held_as)


def setup_inputs(seed: int = 0) -> dict:
    key_of = jax.random.split(jax.random.key(seed), 11)
    right_side = bell_draw(key_of[0], (PLANES, PLANE_CLUSTERS, OBJECTIVES, BLOCK), 1.0, 6.0, ((0, 8), (1, 16)), jnp.float32)
    inverse_diag = bell_draw(key_of[1], (PLANES, PLANE_CLUSTERS, BLOCK, BLOCK), BLOCK ** -0.5, 0.25, ((0, 8), (1, 16)))
    back_blocks = bell_draw(key_of[2], (PLANES, PLANE_CLUSTERS, COUPLED, BLOCK, BLOCK), (COUPLED * BLOCK * 3 // 2) ** -0.5, 0.125, ((0, 8), (1, 16)))
    back_near = plant(jax.random.randint(key_of[3], (PLANES, PLANE_CLUSTERS, COUPLED), 0, 3 * CLUSTERS), jax.random.fold_in(key_of[3], 1), 0, (3 * CLUSTERS) - 1).astype(jnp.int32)
    fore_blocks = bell_draw(key_of[4], (PLANES, PLANE_CLUSTERS, COUPLED, BLOCK, BLOCK), (COUPLED * BLOCK * 3 // 2) ** -0.5, 0.125, ((0, 8), (1, 16)))
    fore_near = plant(jax.random.randint(key_of[5], (PLANES, PLANE_CLUSTERS, COUPLED), 0, 3 * CLUSTERS), jax.random.fold_in(key_of[5], 1), 0, (3 * CLUSTERS) - 1).astype(jnp.int32)
    fringe_blocks = bell_draw(key_of[6], (PLANES, ALL_LINKS, BLOCK, BLOCK), BLOCK ** -0.5, 0.25, ((0, 8), (1, 16)))
    fringe_donor = plant(jax.random.randint(key_of[7], (PLANES, ALL_LINKS), 0, CLUSTERS), jax.random.fold_in(key_of[7], 1), 0, CLUSTERS - 1).astype(jnp.int32)
    fringe_dest_keys = jax.random.split(jax.random.fold_in(key_of[8], 1), PLANES * ALL_LINKS // LINKS)
    fringe_dest_turns = jax.random.permutation(jax.random.fold_in(key_of[8], 3), PLANES * ALL_LINKS // LINKS)
    fringe_dest = jax.vmap(lambda own, number: deal_out(jax.random.fold_in(key_of[8], 2), own, number, LINKS, N_DOM, 1, CAPACITY, 2))(fringe_dest_keys, fringe_dest_turns).reshape((PLANES, ALL_LINKS, 1))
    fringe_slot = plant(jax.random.randint(key_of[9], (PLANES, ALL_LINKS), 0, CLUSTERS), jax.random.fold_in(key_of[9], 1), 0, CLUSTERS - 1).astype(jnp.int32)
    return {"right_side": right_side, "inverse_diag": inverse_diag, "back_blocks": back_blocks, "back_near": back_near, "fore_blocks": fore_blocks, "fore_near": fore_near, "fringe_blocks": fringe_blocks, "fringe_donor": fringe_donor, "fringe_dest": fringe_dest, "fringe_slot": fringe_slot}


def neighbours(relative):
    cluster_ids = jnp.arange(PLANE_CLUSTERS, dtype=jnp.int32)
    first_ids = (cluster_ids // CLUSTERS - 1) * CLUSTERS
    return jnp.clip(first_ids[:, None] + relative, 0, PLANE_CLUSTERS - 1).astype(jnp.int32)


def couple(vectors, chosen, blocks):
    picked = vectors[chosen].astype(jnp.float32)
    return jnp.einsum("csoi,csij->coj", picked, blocks.astype(jnp.float32))


def solve_block(vectors, inverse):
    return jnp.einsum("coi,cij->coj", vectors.astype(jnp.float32), inverse.astype(jnp.float32))


def reference(right_side, inverse_diag, back_blocks, back_near, fore_blocks, fore_near, fringe_blocks, fringe_donor, fringe_dest, fringe_slot):
    previous = jnp.zeros((PLANE_CLUSTERS, OBJECTIVES, BLOCK), jnp.bfloat16)
    forward = []
    for plane_at in range(PLANES):
        coupled = couple(previous, neighbours(back_near[plane_at]), back_blocks[plane_at])
        reduced = (right_side[plane_at] - coupled).astype(jnp.bfloat16)
        previous = solve_block(reduced, inverse_diag[plane_at]).astype(jnp.bfloat16)
        forward.append(previous)
    holders = jnp.arange(ALL_LINKS, dtype=jnp.int32) // LINKS
    following = jnp.zeros((PLANE_CLUSTERS, OBJECTIVES, BLOCK), jnp.bfloat16)
    result = [None] * PLANES
    for plane_at in reversed(range(PLANES)):
        donors = (holders * CLUSTERS + fringe_donor[plane_at]).astype(jnp.int32)
        products = jnp.einsum("loi,lij->loj", forward[plane_at][donors].astype(jnp.float32), fringe_blocks[plane_at].astype(jnp.float32)).astype(jnp.bfloat16)
        receptors = (fringe_dest[plane_at][:, 0] * CLUSTERS + fringe_slot[plane_at]).astype(jnp.int32)
        fringe = jnp.zeros((PLANE_CLUSTERS, OBJECTIVES, BLOCK), jnp.float32).at[receptors].add(products.astype(jnp.float32))
        carried = (fringe + couple(following, neighbours(fore_near[plane_at]), fore_blocks[plane_at])).astype(jnp.bfloat16)
        following = (forward[plane_at].astype(jnp.float32) - solve_block(carried, inverse_diag[plane_at])).astype(jnp.bfloat16)
        result[plane_at] = following
    return jnp.stack(result)
```

```python
import functools

import jax
import jax.numpy as jnp
from jax import lax
from jax.experimental import pallas as pl
from jax.experimental.pallas import tpu as pltpu
from jax.sharding import PartitionSpec as P

BF, F32 = jnp.bfloat16, jnp.float32
MESH = pl.DeviceIdType.MESH
PIECES = 4
ROWS = 16


def dot(a, b):
    return jnp.dot(a, b, preferred_element_type=F32)


def kernel(
    rhs_h, diag_h, back_h, fore_h, link_h, back_near, fore_near, donor, dest, slot,
    out,
    rhs, diag, back, fore, link, coup, base, w, xs, prod, pack, part, first, second,
    pick,
    near_u0, near_u1, near_u2, near_u3, near_d0, near_d1, near_d2, near_d3,
    load_sem, up_s, up_r, dn_s, dn_r, f1_s, f1_r, f2_s, f2_r,
):
    p, d = lax.axis_index("plane"), lax.axis_index("dom")
    x, y = d // 4, d % 4
    near_u = (near_u0, near_u1, near_u2, near_u3)
    near_d = (near_d0, near_d1, near_d2, near_d3)
    links = link.shape[0]

    loads = [
        pltpu.make_async_copy(h.at[0], v, load_sem.at[i])
        for i, (h, v) in enumerate(
            ((rhs_h, rhs), (diag_h, diag), (back_h, back), (link_h, link), (fore_h, fore))
        )
    ]
    load_rhs, load_diag, load_back, load_link, load_fore = loads
    load_rhs.start()
    load_diag.start()
    load_back.start()

    barrier = pltpu.get_barrier_semaphore()

    def greet(plane, dom):
        pl.semaphore_signal(
            barrier, inc=1, device_id={"plane": plane, "dom": dom}, device_id_type=MESH
        )

    for step in (-1, 1):
        @pl.when((p + step >= 0) & (p + step < 8))
        def _():
            greet(p + step, d)

            @pl.when(d > 0)
            def _():
                greet(p + step, d - 1)

            @pl.when(d < 15)
            def _():
                greet(p + step, d + 1)

    for j in (1, 2, 3):
        greet(p, x * 4 + (y + j) % 4)
        greet(p, ((x + j) % 4) * 4 + y)
    beside = jnp.where((d > 0) & (d < 15), 3, 2)
    planes = jnp.where((p > 0) & (p < 7), 2, 1)

    def moves(k, step, src, near, ss, rs):
        def one(n, shift):
            return pltpu.make_async_remote_copy(
                src_ref=src.at[k],
                dst_ref=near[k].at[pl.ds(2 - 2 * shift, 2)],
                send_sem=ss.at[k, n],
                recv_sem=rs.at[k, n],
                device_id={"plane": p + step, "dom": d + shift},
                device_id_type=MESH,
            )

        return one(0, 1), one(1, -1), one(2, 0)

    def move(act, k, step, src, near, ss, rs):
        right, left, same = moves(k, step, src, near, ss, rs)
        if act == "recv":
            pl.when(d > 0)(right.wait_recv)
            pl.when(d < 15)(left.wait_recv)
            same.wait_recv()
        else:
            do = (lambda c: c.start()) if act == "start" else (lambda c: c.wait_send())
            pl.when(d < 15)(lambda: do(right))
            pl.when(d > 0)(lambda: do(left))
            do(same)

    up = functools.partial(move, step=1, src=w, near=near_u, ss=up_s, rs=up_r)
    down = functools.partial(move, step=-1, src=xs, near=near_d, ss=dn_s, rs=dn_r)

    def spot(table, c, s):
        start = (d - 1) * 2
        return jnp.clip(start + table[0, c, s], 0, 31) - start

    load_rhs.wait()
    load_diag.wait()
    for c in range(2):
        whole = dot(rhs[c].astype(BF), diag[c])
        for k in range(PIECES):
            base[k, c] = whole[k * ROWS:(k + 1) * ROWS]

    pl.semaphore_wait(barrier, beside * planes + 6)

    @pl.when(p == 0)
    def _():
        for k in range(PIECES):
            w[k] = base[k].astype(BF)
            up("start", k)

    load_back.wait()
    load_link.start()
    load_fore.start()

    def compose(src, dst):
        def body(i, _):
            dst[i // 2, i % 2] = dot(src[i // 2, i % 2], diag[i // 2]).astype(BF)
            return 0

        lax.fori_loop(0, 4, body, 0)

    pl.when(p > 0)(lambda: compose(back, coup))

    def choose(i, _):
        one, two = jnp.int32(links), jnp.int32(links)
        for l in range(links):
            hit = dest[0, l] * 2 + slot[0, l] == i
            two = jnp.where(hit & (one < links), l, two)
            one = jnp.where(hit & (one == links), l, one)
        pick[0, i] = one
        pick[1, i] = two
        return 0

    lax.fori_loop(0, 32, choose, 0)
    for k in range(PIECES):
        prod[k, links] = jnp.zeros((ROWS, 640), BF)

    @pl.when(p >= 3)
    def _():
        load_fore.wait()
        pl.when(p < 7)(lambda: compose(fore, back))

    def up_step(k):
        up("recv", k)
        for c in range(2):
            total = base[k, c]
            for s in range(2):
                total = total - dot(near_u[k][spot(back_near, c, s)], coup[c, s])
            w[k, c] = total.astype(BF)

    def products(ks):
        def body(l, _):
            rows = jnp.concatenate([w[k, donor[0, l]] for k in ks], axis=0)
            got = dot(rows, link[l]).astype(BF)
            for i, k in enumerate(ks):
                prod[k, l] = got[i * ROWS:(i + 1) * ROWS]
            return 0

        lax.fori_loop(0, links, body, 0)

    def phase1(k):
        a = y if k % 2 == 0 else x
        found = []
        for j in (1, 2, 3):
            there = (a + j) % 4
            target = x * 4 + there if k % 2 == 0 else there * 4 + y
            found.append(pltpu.make_async_remote_copy(
                src_ref=pack.at[k, there],
                dst_ref=first.at[k, j - 1],
                send_sem=f1_s.at[k, j - 1],
                recv_sem=f1_r.at[k, j - 1],
                device_id={"plane": p, "dom": target},
                device_id_type=MESH,
            ))
        return a, found

    def phase2(k):
        b = x if k % 2 == 0 else y
        found = []
        for j in (1, 2, 3):
            there = (b + j) % 4
            target = there * 4 + y if k % 2 == 0 else x * 4 + there
            found.append(pltpu.make_async_remote_copy(
                src_ref=part.at[k, there],
                dst_ref=second.at[k, j - 1],
                send_sem=f2_s.at[k, j - 1],
                recv_sem=f2_r.at[k, j - 1],
                device_id={"plane": p, "dom": target},
                device_id_type=MESH,
            ))
        return b, found

    def send_first(k):
        def body(i, _):
            a, b, c = i // 8, (i // 2) % 4, i % 2
            cell = (b * 4 + a) * 2 + c if k % 2 == 0 else i
            both = prod[k, pick[0, cell]].astype(F32) + prod[k, pick[1, cell]].astype(F32)
            pack[k, a, b, c] = both.astype(BF)
            return 0

        lax.fori_loop(0, 32, body, 0)
        for copy in phase1(k)[1]:
            copy.start()

    def send_second(k):
        a, copies = phase1(k)
        for copy in copies:
            copy.wait_recv()

        def body(b, _):
            for c in range(2):
                total = pack[k, a, b, c].astype(F32)
                for j in range(3):
                    total = total + first[k, j, b, c].astype(F32)
                part[k, b, c] = total.astype(BF)
            return 0

        lax.fori_loop(0, 4, body, 0)
        for copy in phase2(k)[1]:
            copy.start()

    def settle(k):
        b, copies = phase2(k)
        for copy in copies:
            copy.wait_recv()
        for c in range(2):
            total = part[k, b, c].astype(F32)
            for j in range(3):
                total = total + second[k, j, c].astype(F32)
            base[k, c] = w[k, c].astype(F32) - dot(total.astype(BF), diag[c])

    def finish(k, c, value):
        value = value.astype(BF)
        xs[k, c] = value
        out[0, c, k * ROWS:(k + 1) * ROWS] = value

    def turn(k):
        for c in range(2):
            finish(k, c, base[k, c])
        down("start", k)

    def down_step(k):
        down("recv", k)
        for c in range(2):
            total = base[k, c]
            for s in range(2):
                total = total - dot(near_d[k][spot(fore_near, c, s)], back[c, s])
            finish(k, c, total)
        pl.when(p > 0)(lambda: down("start", k))

    @pl.when(p == 7)
    def _():
        load_link.wait()
        for k in range(PIECES):
            up_step(k)
            products((k,))
            send_first(k)
            if k >= 2:
                send_second(k - 2)
        for k in range(PIECES):
            settle(k)
            turn(k)
            if k < 2:
                send_second(k + 2)

    @pl.when(p < 7)
    def _():
        @pl.when(p > 0)
        def _():
            for k in range(PIECES):
                up_step(k)
                up("start", k)

        load_link.wait()
        products(tuple(range(PIECES)))
        for k in range(PIECES):
            send_first(k)
        for k in range(PIECES):
            send_second(k)

        @pl.when(p < 3)
        def _():
            load_fore.wait()
            compose(fore, back)

        for k in range(PIECES):
            settle(k)
            down_step(k)

    for k in range(PIECES):
        pl.when(p < 7)(lambda: up("sent", k))
        pl.when(p > 0)(lambda: down("sent", k))
        for copy in phase1(k)[1] + phase2(k)[1]:
            copy.wait_send()


def local(rhs, diag, back, back_near, fore, fore_near, link, donor, dest, slot):
    links = link.shape[1]
    piece = (PIECES, 2, ROWS, 640)
    near = pltpu.VMEM((6, ROWS, 640), BF)
    sems = pltpu.SemaphoreType.DMA((PIECES, 3))
    anywhere = pl.BlockSpec(memory_space=pl.ANY)
    scalars = pl.BlockSpec(memory_space=pltpu.SMEM)
    return pl.pallas_call(
        kernel,
        out_shape=jax.ShapeDtypeStruct(rhs.shape, BF),
        in_specs=[anywhere] * 5 + [scalars] * 5,
        out_specs=pl.BlockSpec(memory_space=pltpu.VMEM),
        scratch_shapes=[
            pltpu.VMEM(rhs.shape[1:], F32),
            pltpu.VMEM(diag.shape[1:], BF),
            pltpu.VMEM(back.shape[1:], BF),
            pltpu.VMEM(fore.shape[1:], BF),
            pltpu.VMEM(link.shape[1:], BF),
            pltpu.VMEM(back.shape[1:], BF),
            pltpu.VMEM(piece, F32),
            pltpu.VMEM(piece, BF),
            pltpu.VMEM(piece, BF),
            pltpu.VMEM((PIECES, links + 1, ROWS, 640), BF),
            pltpu.VMEM((PIECES, 4, 4, 2, ROWS, 640), BF),
            pltpu.VMEM((PIECES, 4, 2, ROWS, 640), BF),
            pltpu.VMEM((PIECES, 3, 4, 2, ROWS, 640), BF),
            pltpu.VMEM((PIECES, 3, 2, ROWS, 640), BF),
            pltpu.SMEM((2, 32), jnp.int32),
        ]
        + [near] * (2 * PIECES)
        + [pltpu.SemaphoreType.DMA((5,))]
        + [sems] * 8,
        compiler_params=pltpu.CompilerParams(
            collective_id=0, has_side_effects=True, vmem_limit_bytes=58 * 1024 * 1024
        ),
        cost_estimate=pl.CostEstimate(
            flops=2 * 32 * 640 * 640 * 640, bytes_accessed=20_000_000, transcendentals=0
        ),
    )(rhs, diag, back, fore, link, back_near, fore_near, donor, dest[:, :, 0], slot)


def solution(mesh):
    return jax.shard_map(
        local,
        mesh=mesh,
        in_specs=(
            P("plane", "dom", None, None),
            P("plane", "dom", None, None),
            P("plane", "dom", None, None, None),
            P("plane", "dom", None),
            P("plane", "dom", None, None, None),
            P("plane", "dom", None),
            P("plane", "dom", None, None),
            P("plane", "dom"),
            P("plane", "dom", None),
            P("plane", "dom"),
        ),
        out_specs=P("plane", "dom", None, None),
        check_vma=False,
    )
```

```python
import functools

import jax
import jax.numpy as jnp
from jax import lax
from jax.experimental import pallas as pl
from jax.experimental.pallas import tpu as pltpu
from jax.sharding import PartitionSpec as P

BF, F32 = jnp.bfloat16, jnp.float32
MESH = pl.DeviceIdType.MESH
PIECES = 4
ROWS = 16


def dot(a, b):
    return jnp.dot(a, b, preferred_element_type=F32)


def kernel(
    rhs_h, diag_h, back_h, fore_h, link_h, back_near, fore_near, donor, dest, slot,
    out,
    rhs, diag, back, fore, link, coup, base, w, xs, prod, pack, part, first, second,
    pick,
    near_u0, near_u1, near_u2, near_u3, near_d0, near_d1, near_d2, near_d3,
    load_sem, up_s, up_r, dn_s, dn_r, f1_s, f1_r, f2_s, f2_r, go_sem,
):
    p, d = lax.axis_index("plane"), lax.axis_index("dom")
    x, y = d // 4, d % 4
    near_u = (near_u0, near_u1, near_u2, near_u3)
    near_d = (near_d0, near_d1, near_d2, near_d3)
    links = link.shape[0]

    loads = [
        pltpu.make_async_copy(h.at[0], v, load_sem.at[i])
        for i, (h, v) in enumerate(
            ((rhs_h, rhs), (diag_h, diag), (back_h, back), (link_h, link), (fore_h, fore))
        )
    ]
    load_rhs, load_diag, load_back, load_link, load_fore = loads
    load_diag.start()

    @pl.when(p > 0)
    def _():
        load_back.start()

    load_rhs.start()

    barrier = pltpu.get_barrier_semaphore()

    def greet(plane, dom):
        pl.semaphore_signal(
            barrier, inc=1, device_id={"plane": plane, "dom": dom}, device_id_type=MESH
        )

    for step in (-1, 1):
        @pl.when((p + step >= 0) & (p + step < 8))
        def _():
            greet(p + step, d)

            @pl.when(d > 0)
            def _():
                greet(p + step, d - 1)

            @pl.when(d < 15)
            def _():
                greet(p + step, d + 1)

    for j in (1, 2, 3):
        greet(p, x * 4 + (y + j) % 4)
        greet(p, ((x + j) % 4) * 4 + y)
    beside = jnp.where((d > 0) & (d < 15), 3, 2)
    planes = jnp.where((p > 0) & (p < 7), 2, 1)

    def move(act, k, c, step, src, near, ss, rs):
        def one(n, shift):
            return pltpu.make_async_remote_copy(
                src_ref=src.at[k, c],
                dst_ref=near[k].at[2 - 2 * shift + c],
                send_sem=ss.at[k, c, n],
                recv_sem=rs.at[k, c, n],
                device_id={"plane": p + step, "dom": d + shift},
                device_id_type=MESH,
            )

        right, left, same = one(0, 1), one(1, -1), one(2, 0)
        if act == "recv":
            pl.when(d > 0)(right.wait_recv)
            pl.when(d < 15)(left.wait_recv)
            same.wait_recv()
        else:
            do = (lambda m: m.start()) if act == "start" else (lambda m: m.wait_send())
            pl.when(d < 15)(lambda: do(right))
            pl.when(d > 0)(lambda: do(left))
            do(same)

    up = functools.partial(move, step=1, src=w, near=near_u, ss=up_s, rs=up_r)
    down = functools.partial(move, step=-1, src=xs, near=near_d, ss=dn_s, rs=dn_r)

    def spot(table, c, s):
        start = (d - 1) * 2
        return jnp.clip(start + table[0, c, s], 0, 31) - start

    def compose(src, dst):
        def body(i, _):
            dst[i // 2, i % 2] = dot(src[i // 2, i % 2], diag[i // 2]).astype(BF)
            return 0

        lax.fori_loop(0, 4, body, 0)

    load_diag.wait()

    @pl.when(p > 0)
    def _():
        load_back.wait()
        compose(back, coup)

    load_rhs.wait()
    for c in range(2):
        whole = dot(rhs[c].astype(BF), diag[c])
        for k in range(PIECES):
            base[k, c] = whole[k * ROWS:(k + 1) * ROWS]

    pl.semaphore_wait(barrier, beside * planes + 6)

    @pl.when(p == 0)
    def _():
        for k in range(PIECES):
            for c in range(2):
                w[k, c] = base[k, c].astype(BF)
                up("start", k, c)

    load_link.start()
    load_fore.start()

    def choose(i, _):
        one, two = jnp.int32(links), jnp.int32(links)
        for l in range(links):
            hit = dest[0, l] * 2 + slot[0, l] == i
            two = jnp.where(hit & (one < links), l, two)
            one = jnp.where(hit & (one == links), l, one)
        pick[0, i] = one
        pick[1, i] = two
        return 0

    def ready():
        lax.fori_loop(0, 32, choose, 0)
        for k in range(PIECES):
            prod[k, links] = jnp.zeros((ROWS, 640), BF)
        load_fore.wait()
        pl.when(p < 7)(lambda: compose(fore, back))

    pl.when(p >= 3)(ready)

    def up_step(k, send=False):
        for c in range(2):
            up("recv", k, c)
        for c in range(2):
            total = base[k, c]
            for s in range(2):
                total = total - dot(near_u[k][spot(back_near, c, s)], coup[c, s])
            w[k, c] = total.astype(BF)
            if send:
                up("start", k, c)

    def products(ks):
        def body(l, _):
            rows = jnp.concatenate([w[k, donor[0, l]] for k in ks], axis=0)
            got = dot(rows, link[l]).astype(BF)
            for i, k in enumerate(ks):
                prod[k, l] = got[i * ROWS:(i + 1) * ROWS]
            return 0

        lax.fori_loop(0, links, body, 0, unroll=4)

    def phase1(k):
        a = y if k % 2 == 0 else x
        found = []
        for j in (1, 2, 3):
            there = (a + j) % 4
            target = x * 4 + there if k % 2 == 0 else there * 4 + y
            found.append(pltpu.make_async_remote_copy(
                src_ref=pack.at[k, there],
                dst_ref=first.at[k, j - 1],
                send_sem=f1_s.at[k, j - 1],
                recv_sem=f1_r.at[k, j - 1],
                device_id={"plane": p, "dom": target},
                device_id_type=MESH,
            ))
        return a, found

    def phase2(k):
        b = x if k % 2 == 0 else y
        found = []
        for j in (1, 2, 3):
            there = (b + j) % 4
            target = there * 4 + y if k % 2 == 0 else x * 4 + there
            found.append(pltpu.make_async_remote_copy(
                src_ref=part.at[k, there],
                dst_ref=second.at[k, j - 1],
                send_sem=f2_s.at[k, j - 1],
                recv_sem=f2_r.at[k, j - 1],
                device_id={"plane": p, "dom": target},
                device_id_type=MESH,
            ))
        return b, found

    def send_first(k):
        def body(i, _):
            a, b, c = i // 8, (i // 2) % 4, i % 2
            cell = (b * 4 + a) * 2 + c if k % 2 == 0 else i
            both = prod[k, pick[0, cell]].astype(F32) + prod[k, pick[1, cell]].astype(F32)
            pack[k, a, b, c] = both.astype(BF)
            return 0

        lax.fori_loop(0, 32, body, 0, unroll=8)
        for copy in phase1(k)[1]:
            copy.start()

    def send_second(k):
        a, copies = phase1(k)
        for copy in copies:
            copy.wait_recv()

        def body(b, _):
            for c in range(2):
                total = pack[k, a, b, c].astype(F32)
                for j in range(3):
                    total = total + first[k, j, b, c].astype(F32)
                part[k, b, c] = total.astype(BF)
            return 0

        lax.fori_loop(0, 4, body, 0, unroll=2)
        for copy in phase2(k)[1]:
            copy.start()

    def settle(k):
        b, copies = phase2(k)
        for copy in copies:
            copy.wait_recv()
        for c in range(2):
            total = part[k, b, c].astype(F32)
            for j in range(3):
                total = total + second[k, j, c].astype(F32)
            base[k, c] = w[k, c].astype(F32) - dot(total.astype(BF), diag[c])

    def finish(k, c, value):
        value = value.astype(BF)
        xs[k, c] = value
        out[0, c, k * ROWS:(k + 1) * ROWS] = value

    def turn(k):
        for c in range(2):
            finish(k, c, base[k, c])
            down("start", k, c)

    def down_step(k):
        for c in range(2):
            down("recv", k, c)
        for c in range(2):
            total = base[k, c]
            for s in range(2):
                total = total - dot(near_d[k][spot(fore_near, c, s)], back[c, s])
            finish(k, c, total)
            pl.when(p > 0)(lambda: down("start", k, c))

    @pl.when(p == 7)
    def _():
        load_link.wait()
        for k in (0, 2):
            up_step(k)
            up_step(k + 1)
            products((k, k + 1))
            send_first(k)
            send_first(k + 1)
        pl.semaphore_signal(
            go_sem, inc=1, device_id={"plane": p - 1, "dom": d}, device_id_type=MESH
        )
        send_second(0)
        send_second(1)
        for k in range(PIECES):
            settle(k)
            turn(k)
            if k < 2:
                send_second(k + 2)

    @pl.when(p < 7)
    def _():
        @pl.when(p > 0)
        def _():
            for k in range(PIECES):
                up_step(k, True)

        pl.when(p < 3)(ready)
        load_link.wait()
        products(tuple(range(PIECES)))
        for k in range(PIECES):
            if k == 2:
                pl.when(p == 6)(lambda: pl.semaphore_wait(go_sem, 1))
            send_first(k)
        for k in range(PIECES):
            send_second(k)

        for k in range(PIECES):
            settle(k)
            down_step(k)

    for k in range(PIECES):
        for c in range(2):
            pl.when(p < 7)(lambda: up("sent", k, c))
            pl.when(p > 0)(lambda: down("sent", k, c))
        for copy in phase1(k)[1] + phase2(k)[1]:
            copy.wait_send()


def local(rhs, diag, back, back_near, fore, fore_near, link, donor, dest, slot):
    links = link.shape[1]
    piece = (PIECES, 2, ROWS, 640)
    near = pltpu.VMEM((6, ROWS, 640), BF)
    each = pltpu.SemaphoreType.DMA((PIECES, 2, 3))
    sems = pltpu.SemaphoreType.DMA((PIECES, 3))
    anywhere = pl.BlockSpec(memory_space=pl.ANY)
    scalars = pl.BlockSpec(memory_space=pltpu.SMEM)
    return pl.pallas_call(
        kernel,
        out_shape=pltpu.VMEM(rhs.shape, BF),
        in_specs=[anywhere] * 5 + [scalars] * 5,
        out_specs=pl.BlockSpec(memory_space=pltpu.VMEM),
        scratch_shapes=[
            pltpu.VMEM(rhs.shape[1:], F32),
            pltpu.VMEM(diag.shape[1:], BF),
            pltpu.VMEM(back.shape[1:], BF),
            pltpu.VMEM(fore.shape[1:], BF),
            pltpu.VMEM(link.shape[1:], BF),
            pltpu.VMEM(back.shape[1:], BF),
            pltpu.VMEM(piece, F32),
            pltpu.VMEM(piece, BF),
            pltpu.VMEM(piece, BF),
            pltpu.VMEM((PIECES, links + 1, ROWS, 640), BF),
            pltpu.VMEM((PIECES, 4, 4, 2, ROWS, 640), BF),
            pltpu.VMEM((PIECES, 4, 2, ROWS, 640), BF),
            pltpu.VMEM((PIECES, 3, 4, 2, ROWS, 640), BF),
            pltpu.VMEM((PIECES, 3, 2, ROWS, 640), BF),
            pltpu.SMEM((2, 32), jnp.int32),
        ]
        + [near] * (2 * PIECES)
        + [pltpu.SemaphoreType.DMA((5,))]
        + [each] * 4
        + [sems] * 4
        + [pltpu.SemaphoreType.REGULAR],
        compiler_params=pltpu.CompilerParams(
            collective_id=0, has_side_effects=True, vmem_limit_bytes=58 * 1024 * 1024
        ),
        cost_estimate=pl.CostEstimate(
            flops=2 * 32 * 640 * 640 * 640, bytes_accessed=20_000_000, transcendentals=0
        ),
    )(rhs, diag, back, fore, link, back_near, fore_near, donor, dest[:, :, 0], slot)


def solution(mesh):
    return jax.shard_map(
        local,
        mesh=mesh,
        in_specs=(
            P("plane", "dom", None, None),
            P("plane", "dom", None, None),
            P("plane", "dom", None, None, None),
            P("plane", "dom", None),
            P("plane", "dom", None, None, None),
            P("plane", "dom", None),
            P("plane", "dom", None, None),
            P("plane", "dom"),
            P("plane", "dom", None),
            P("plane", "dom"),
        ),
        out_specs=P("plane", "dom", None, None),
        check_vma=False,
    )
```

```python
import functools

import jax
import jax.numpy as jnp
from jax import lax
from jax.experimental import pallas as pl
from jax.experimental.pallas import tpu as pltpu
from jax.sharding import PartitionSpec as P

BF, F32 = jnp.bfloat16, jnp.float32
MESH = pl.DeviceIdType.MESH
PIECES = 4
ROWS = 16


def dot(a, b):
    return jnp.dot(a, b, preferred_element_type=F32)


def kernel(
    rhs_h, diag_h, back_h, fore_h, link_h, back_near, fore_near, donor, dest, slot,
    out,
    rhs, diag, back, fore, link, coup, base, w, xs, prod, pack, part, first, second,
    pick,
    near_u0, near_u1, near_u2, near_u3, near_d0, near_d1, near_d2, near_d3,
    load_sem, up_s, up_r, dn_s, dn_r, f1_s, f1_r, f2_s, f2_r, go_sem,
):
    p, d = lax.axis_index("plane"), lax.axis_index("dom")
    x, y = d // 4, d % 4
    near_u = (near_u0, near_u1, near_u2, near_u3)
    near_d = (near_d0, near_d1, near_d2, near_d3)
    links = link.shape[0]

    loads = [
        pltpu.make_async_copy(h.at[0], v, load_sem.at[i])
        for i, (h, v) in enumerate(
            ((rhs_h, rhs), (diag_h, diag), (back_h, back), (link_h, link), (fore_h, fore))
        )
    ]
    load_rhs, load_diag, load_back, load_link, load_fore = loads
    load_diag.start()

    @pl.when(p > 0)
    def _():
        load_back.start()

    load_rhs.start()

    barrier = pltpu.get_barrier_semaphore()

    def greet(plane, dom):
        pl.semaphore_signal(
            barrier, inc=1, device_id={"plane": plane, "dom": dom}, device_id_type=MESH
        )

    for step in (-1, 1):
        @pl.when((p + step >= 0) & (p + step < 8))
        def _():
            greet(p + step, d)

            @pl.when(d > 0)
            def _():
                greet(p + step, d - 1)

            @pl.when(d < 15)
            def _():
                greet(p + step, d + 1)

    for j in (1, 2, 3):
        greet(p, x * 4 + (y + j) % 4)
        greet(p, ((x + j) % 4) * 4 + y)
    beside = jnp.where((d > 0) & (d < 15), 3, 2)
    planes = jnp.where((p > 0) & (p < 7), 2, 1)

    def move(act, k, c, step, src, near, ss, rs):
        def one(n, shift):
            return pltpu.make_async_remote_copy(
                src_ref=src.at[k, c],
                dst_ref=near[k].at[2 - 2 * shift + c],
                send_sem=ss.at[k, c, n],
                recv_sem=rs.at[k, c, n],
                device_id={"plane": p + step, "dom": d + shift},
                device_id_type=MESH,
            )

        right, left, same = one(0, 1), one(1, -1), one(2, 0)
        if act == "recv":
            pl.when(d > 0)(right.wait_recv)
            pl.when(d < 15)(left.wait_recv)
            same.wait_recv()
        else:
            do = (lambda m: m.start()) if act == "start" else (lambda m: m.wait_send())
            pl.when(d < 15)(lambda: do(right))
            pl.when(d > 0)(lambda: do(left))
            do(same)

    up = functools.partial(move, step=1, src=w, near=near_u, ss=up_s, rs=up_r)
    down = functools.partial(move, step=-1, src=xs, near=near_d, ss=dn_s, rs=dn_r)

    def spot(table, c, s):
        start = (d - 1) * 2
        return jnp.clip(start + table[0, c, s], 0, 31) - start

    def compose(src, dst):
        def body(i, _):
            dst[i // 2, i % 2] = dot(src[i // 2, i % 2], diag[i // 2]).astype(BF)
            return 0

        lax.fori_loop(0, 4, body, 0)

    load_diag.wait()

    @pl.when(p > 0)
    def _():
        load_back.wait()
        compose(back, coup)

    load_rhs.wait()
    for c in range(2):
        whole = dot(rhs[c].astype(BF), diag[c])
        for k in range(PIECES):
            base[k, c] = whole[k * ROWS:(k + 1) * ROWS]

    pl.semaphore_wait(barrier, beside * planes + 6)

    @pl.when(p == 0)
    def _():
        for k in range(PIECES):
            for c in range(2):
                w[k, c] = base[k, c].astype(BF)
                up("start", k, c)

    load_link.start()
    load_fore.start()

    def choose(i, _):
        one, two = jnp.int32(links), jnp.int32(links)
        for l in range(links):
            hit = dest[0, l] * 2 + slot[0, l] == i
            two = jnp.where(hit & (one < links), l, two)
            one = jnp.where(hit & (one == links), l, one)
        pick[0, i] = one
        pick[1, i] = two
        return 0

    def ready():
        lax.fori_loop(0, 32, choose, 0)
        for k in range(PIECES):
            prod[k, links] = jnp.zeros((ROWS, 640), BF)
        load_fore.wait()
        pl.when(p < 7)(lambda: compose(fore, back))

    pl.when(p >= 3)(ready)

    def up_step(k, send=False):
        for c in range(2):
            up("recv", k, c)
        for c in range(2):
            total = base[k, c]
            for s in range(2):
                total = total - dot(near_u[k][spot(back_near, c, s)], coup[c, s])
            w[k, c] = total.astype(BF)
            if send:
                up("start", k, c)

    def products(ks):
        def body(l, _):
            rows = jnp.concatenate([w[k, donor[0, l]] for k in ks], axis=0)
            got = dot(rows, link[l]).astype(BF)
            for i, k in enumerate(ks):
                prod[k, l] = got[i * ROWS:(i + 1) * ROWS]
            return 0

        lax.fori_loop(0, links, body, 0, unroll=4)

    def phase1(k):
        a = y if k % 2 == 0 else x
        found = []
        for j in (1, 2, 3):
            there = (a + j) % 4
            target = x * 4 + there if k % 2 == 0 else there * 4 + y
            found.append(pltpu.make_async_remote_copy(
                src_ref=pack.at[k, there],
                dst_ref=first.at[k, j - 1],
                send_sem=f1_s.at[k, j - 1],
                recv_sem=f1_r.at[k, j - 1],
                device_id={"plane": p, "dom": target},
                device_id_type=MESH,
            ))
        return a, found

    def phase2(k):
        b = x if k % 2 == 0 else y
        found = []
        for j in (1, 2, 3):
            there = (b + j) % 4
            target = there * 4 + y if k % 2 == 0 else x * 4 + there
            found.append(pltpu.make_async_remote_copy(
                src_ref=part.at[k, there],
                dst_ref=second.at[k, j - 1],
                send_sem=f2_s.at[k, j - 1],
                recv_sem=f2_r.at[k, j - 1],
                device_id={"plane": p, "dom": target},
                device_id_type=MESH,
            ))
        return b, found

    def send_first(k):
        def body(i, _):
            a, b, c = i // 8, (i // 2) % 4, i % 2
            cell = (b * 4 + a) * 2 + c if k % 2 == 0 else i
            both = prod[k, pick[0, cell]].astype(F32) + prod[k, pick[1, cell]].astype(F32)
            pack[k, a, b, c] = both.astype(BF)
            return 0

        lax.fori_loop(0, 32, body, 0, unroll=8)
        for copy in phase1(k)[1]:
            copy.start()

    def send_second(k):
        a, copies = phase1(k)
        for copy in copies:
            copy.wait_recv()

        def body(b, _):
            for c in range(2):
                total = pack[k, a, b, c].astype(F32)
                for j in range(3):
                    total = total + first[k, j, b, c].astype(F32)
                part[k, b, c] = total.astype(BF)
            return 0

        lax.fori_loop(0, 4, body, 0, unroll=2)
        for copy in phase2(k)[1]:
            copy.start()

    def settle(k):
        b, copies = phase2(k)
        for copy in copies:
            copy.wait_recv()
        for c in range(2):
            total = part[k, b, c].astype(F32)
            for j in range(3):
                total = total + second[k, j, c].astype(F32)
            base[k, c] = w[k, c].astype(F32) - dot(total.astype(BF), diag[c])

    def finish(k, c, value):
        value = value.astype(BF)
        xs[k, c] = value
        out[0, c, k * ROWS:(k + 1) * ROWS] = value

    def turn(k):
        for c in range(2):
            finish(k, c, base[k, c])
            down("start", k, c)

    def down_step(k):
        for c in range(2):
            down("recv", k, c)
        for c in range(2):
            total = base[k, c]
            for s in range(2):
                total = total - dot(near_d[k][spot(fore_near, c, s)], back[c, s])
            finish(k, c, total)
            pl.when(p > 0)(lambda: down("start", k, c))

    @pl.when(p == 7)
    def _():
        load_link.wait()
        for k in (0, 2):
            up_step(k)
            up_step(k + 1)
            products((k, k + 1))
            send_first(k)
            send_first(k + 1)
        send_second(0)
        send_second(1)
        pl.semaphore_signal(
            go_sem, inc=1, device_id={"plane": p - 1, "dom": d}, device_id_type=MESH
        )
        for k in range(PIECES):
            settle(k)
            turn(k)
            if k < 2:
                send_second(k + 2)

    @pl.when(p < 7)
    def _():
        @pl.when(p > 0)
        def _():
            for k in range(PIECES):
                up_step(k, True)

        pl.when(p < 3)(ready)
        load_link.wait()
        products(tuple(range(PIECES)))
        for k in range(PIECES):
            if k == 2:
                pl.when(p == 6)(lambda: pl.semaphore_wait(go_sem, 1))
            send_first(k)
        for k in range(PIECES):
            send_second(k)

        @pl.when(p < 6)
        def _():
            for k in range(PIECES):
                settle(k)

        for k in range(PIECES):
            pl.when(p == 6)(lambda: settle(k))
            down_step(k)

    for k in range(PIECES):
        for c in range(2):
            pl.when(p < 7)(lambda: up("sent", k, c))
            pl.when(p > 0)(lambda: down("sent", k, c))
        for copy in phase1(k)[1] + phase2(k)[1]:
            copy.wait_send()


def local(rhs, diag, back, back_near, fore, fore_near, link, donor, dest, slot):
    links = link.shape[1]
    piece = (PIECES, 2, ROWS, 640)
    near = pltpu.VMEM((6, ROWS, 640), BF)
    each = pltpu.SemaphoreType.DMA((PIECES, 2, 3))
    sems = pltpu.SemaphoreType.DMA((PIECES, 3))
    anywhere = pl.BlockSpec(memory_space=pl.ANY)
    scalars = pl.BlockSpec(memory_space=pltpu.SMEM)
    return pl.pallas_call(
        kernel,
        out_shape=pltpu.VMEM(rhs.shape, BF),
        in_specs=[anywhere] * 5 + [scalars] * 5,
        out_specs=pl.BlockSpec(memory_space=pltpu.VMEM),
        scratch_shapes=[
            pltpu.VMEM(rhs.shape[1:], F32),
            pltpu.VMEM(diag.shape[1:], BF),
            pltpu.VMEM(back.shape[1:], BF),
            pltpu.VMEM(fore.shape[1:], BF),
            pltpu.VMEM(link.shape[1:], BF),
            pltpu.VMEM(back.shape[1:], BF),
            pltpu.VMEM(piece, F32),
            pltpu.VMEM(piece, BF),
            pltpu.VMEM(piece, BF),
            pltpu.VMEM((PIECES, links + 1, ROWS, 640), BF),
            pltpu.VMEM((PIECES, 4, 4, 2, ROWS, 640), BF),
            pltpu.VMEM((PIECES, 4, 2, ROWS, 640), BF),
            pltpu.VMEM((PIECES, 3, 4, 2, ROWS, 640), BF),
            pltpu.VMEM((PIECES, 3, 2, ROWS, 640), BF),
            pltpu.SMEM((2, 32), jnp.int32),
        ]
        + [near] * (2 * PIECES)
        + [pltpu.SemaphoreType.DMA((5,))]
        + [each] * 4
        + [sems] * 4
        + [pltpu.SemaphoreType.REGULAR],
        compiler_params=pltpu.CompilerParams(
            collective_id=0, has_side_effects=True, vmem_limit_bytes=58 * 1024 * 1024
        ),
        cost_estimate=pl.CostEstimate(
            flops=2 * 32 * 640 * 640 * 640, bytes_accessed=20_000_000, transcendentals=0
        ),
    )(rhs, diag, back, fore, link, back_near, fore_near, donor, dest[:, :, 0], slot)


def solution(mesh):
    return jax.shard_map(
        local,
        mesh=mesh,
        in_specs=(
            P("plane", "dom", None, None),
            P("plane", "dom", None, None),
            P("plane", "dom", None, None, None),
            P("plane", "dom", None),
            P("plane", "dom", None, None, None),
            P("plane", "dom", None),
            P("plane", "dom", None, None),
            P("plane", "dom"),
            P("plane", "dom", None),
            P("plane", "dom"),
        ),
        out_specs=P("plane", "dom", None, None),
        check_vma=False,
    )
```

```python
import functools

import jax
import jax.numpy as jnp
from jax import lax
from jax.experimental import pallas as pl
from jax.experimental.pallas import tpu as pltpu
from jax.sharding import PartitionSpec as P

BF, F32 = jnp.bfloat16, jnp.float32
MESH = pl.DeviceIdType.MESH
PIECES = 4
ROWS = 16


def dot(a, b):
    return jnp.dot(a, b, preferred_element_type=F32)


def kernel(
    rhs_h, diag_h, back_h, fore_h, link_h, back_near, fore_near, donor, dest, slot,
    out,
    rhs, diag, back, fore, link, coup, base, w, xs, prod, pack, part, first, second,
    pick,
    near_u0, near_u1, near_u2, near_u3, near_d0, near_d1, near_d2, near_d3,
    load_sem, up_s, up_r, dn_s, dn_r, f1_s, f1_r, f2_s, f2_r, go_sem,
):
    p, d = lax.axis_index("plane"), lax.axis_index("dom")
    x, y = d // 4, d % 4
    near_u = (near_u0, near_u1, near_u2, near_u3)
    near_d = (near_d0, near_d1, near_d2, near_d3)
    links = link.shape[0]

    loads = [
        pltpu.make_async_copy(h.at[0], v, load_sem.at[i])
        for i, (h, v) in enumerate(
            ((rhs_h, rhs), (diag_h, diag), (back_h, back), (link_h, link), (fore_h, fore))
        )
    ]
    load_rhs, load_diag, load_back, load_link, load_fore = loads
    load_diag.start()

    @pl.when(p > 0)
    def _():
        load_back.start()

    load_rhs.start()

    barrier = pltpu.get_barrier_semaphore()

    def greet(plane, dom):
        pl.semaphore_signal(
            barrier, inc=1, device_id={"plane": plane, "dom": dom}, device_id_type=MESH
        )

    for step in (-1, 1):
        @pl.when((p + step >= 0) & (p + step < 8))
        def _():
            greet(p + step, d)

            @pl.when(d > 0)
            def _():
                greet(p + step, d - 1)

            @pl.when(d < 15)
            def _():
                greet(p + step, d + 1)

    for j in (1, 2, 3):
        greet(p, x * 4 + (y + j) % 4)
        greet(p, ((x + j) % 4) * 4 + y)
    beside = jnp.where((d > 0) & (d < 15), 3, 2)
    planes = jnp.where((p > 0) & (p < 7), 2, 1)

    def move(act, k, c, step, src, near, ss, rs):
        def one(n, shift):
            return pltpu.make_async_remote_copy(
                src_ref=src.at[k, c],
                dst_ref=near[k].at[2 - 2 * shift + c],
                send_sem=ss.at[k, c, n],
                recv_sem=rs.at[k, c, n],
                device_id={"plane": p + step, "dom": d + shift},
                device_id_type=MESH,
            )

        right, left, same = one(0, 1), one(1, -1), one(2, 0)
        if act == "recv":
            pl.when(d > 0)(right.wait_recv)
            pl.when(d < 15)(left.wait_recv)
            same.wait_recv()
        else:
            do = (lambda m: m.start()) if act == "start" else (lambda m: m.wait_send())
            pl.when(d < 15)(lambda: do(right))
            pl.when(d > 0)(lambda: do(left))
            do(same)

    up = functools.partial(move, step=1, src=w, near=near_u, ss=up_s, rs=up_r)
    down = functools.partial(move, step=-1, src=xs, near=near_d, ss=dn_s, rs=dn_r)

    def spot(table, c, s):
        start = (d - 1) * 2
        return jnp.clip(start + table[0, c, s], 0, 31) - start

    def compose(src, dst):
        def body(i, _):
            dst[i // 2, i % 2] = dot(src[i // 2, i % 2], diag[i // 2]).astype(BF)
            return 0

        lax.fori_loop(0, 4, body, 0)

    load_diag.wait()

    @pl.when(p > 0)
    def _():
        load_back.wait()
        compose(back, coup)

    load_rhs.wait()
    for c in range(2):
        whole = dot(rhs[c].astype(BF), diag[c])
        for k in range(PIECES):
            base[k, c] = whole[k * ROWS:(k + 1) * ROWS]

    pl.semaphore_wait(barrier, beside * planes + 6)

    @pl.when(p == 0)
    def _():
        for k in range(PIECES):
            for c in range(2):
                w[k, c] = base[k, c].astype(BF)
                up("start", k, c)

    load_link.start()
    load_fore.start()

    def choose(i, _):
        one, two = jnp.int32(links), jnp.int32(links)
        for l in range(links):
            hit = dest[0, l] * 2 + slot[0, l] == i
            two = jnp.where(hit & (one < links), l, two)
            one = jnp.where(hit & (one == links), l, one)
        pick[0, i] = one
        pick[1, i] = two
        return 0

    def ready():
        lax.fori_loop(0, 32, choose, 0)
        for k in range(PIECES):
            prod[k, links] = jnp.zeros((ROWS, 640), BF)
        load_fore.wait()
        pl.when(p < 7)(lambda: compose(fore, back))

    pl.when((p == 3) | (p > 4))(ready)

    def up_step(k, send=False):
        for c in range(2):
            up("recv", k, c)
        for c in range(2):
            total = base[k, c]
            for s in range(2):
                total = total - dot(near_u[k][spot(back_near, c, s)], coup[c, s])
            w[k, c] = total.astype(BF)
            if send:
                up("start", k, c)

    def products(ks):
        def body(l, _):
            rows = jnp.concatenate([w[k, donor[0, l]] for k in ks], axis=0)
            got = dot(rows, link[l]).astype(BF)
            for i, k in enumerate(ks):
                prod[k, l] = got[i * ROWS:(i + 1) * ROWS]
            return 0

        lax.fori_loop(0, links, body, 0, unroll=12)

    def phase1(k):
        a = y if k % 2 == 0 else x
        found = []
        for j in (1, 2, 3):
            there = (a + j) % 4
            target = x * 4 + there if k % 2 == 0 else there * 4 + y
            found.append(pltpu.make_async_remote_copy(
                src_ref=pack.at[k, there],
                dst_ref=first.at[k, j - 1],
                send_sem=f1_s.at[k, j - 1],
                recv_sem=f1_r.at[k, j - 1],
                device_id={"plane": p, "dom": target},
                device_id_type=MESH,
            ))
        return a, found

    def phase2(k):
        b = x if k % 2 == 0 else y
        found = []
        for j in (1, 2, 3):
            there = (b + j) % 4
            target = there * 4 + y if k % 2 == 0 else x * 4 + there
            found.append(pltpu.make_async_remote_copy(
                src_ref=part.at[k, there],
                dst_ref=second.at[k, j - 1],
                send_sem=f2_s.at[k, j - 1],
                recv_sem=f2_r.at[k, j - 1],
                device_id={"plane": p, "dom": target},
                device_id_type=MESH,
            ))
        return b, found

    def send_first(k):
        for i in range(32):
            a, b, c = i // 8, (i // 2) % 4, i % 2
            cell = (b * 4 + a) * 2 + c if k % 2 == 0 else i
            pack[k, a, b, c] = prod[k, pick[0, cell]] + prod[k, pick[1, cell]]
        one, two, three = phase1(k)[1]
        for copy in (one, three, two):
            copy.start()

    def send_second(k):
        a, copies = phase1(k)
        for copy in copies:
            copy.wait_recv()

        for b in range(4):
            for c in range(2):
                total = pack[k, a, b, c].astype(F32)
                for j in range(3):
                    total = total + first[k, j, b, c].astype(F32)
                part[k, b, c] = total.astype(BF)
        one, two, three = phase2(k)[1]
        for copy in (one, three, two):
            copy.start()

    def settle(k):
        b, copies = phase2(k)
        for copy in copies:
            copy.wait_recv()
        for c in range(2):
            total = part[k, b, c].astype(F32)
            for j in range(3):
                total = total + second[k, j, c].astype(F32)
            base[k, c] = w[k, c].astype(F32) - dot(total.astype(BF), diag[c])

    def finish(k, c, value):
        value = value.astype(BF)
        xs[k, c] = value
        out[0, c, k * ROWS:(k + 1) * ROWS] = value

    def turn(k):
        for c in range(2):
            finish(k, c, base[k, c])
            down("start", k, c)

    def down_step(k, send):
        for c in range(2):
            down("recv", k, c)
        for c in range(2):
            total = base[k, c]
            for s in range(2):
                total = total - dot(near_d[k][spot(fore_near, c, s)], back[c, s])
            finish(k, c, total)
            if send:
                down("start", k, c)

    @pl.when(p == 7)
    def _():
        load_link.wait()
        for k in (0, 2):
            up_step(k)
            up_step(k + 1)
            products((k, k + 1))
            send_first(k)
            send_first(k + 1)
        send_second(0)
        send_second(1)
        pl.semaphore_signal(
            go_sem, inc=1, device_id={"plane": p - 1, "dom": d}, device_id_type=MESH
        )
        for k in range(PIECES):
            settle(k)
            turn(k)
            if k < 2:
                send_second(k + 2)

    @pl.when(p < 7)
    def _():
        @pl.when(p > 0)
        def _():
            for k in range(PIECES):
                up_step(k, True)

        pl.when((p < 3) | (p == 4))(ready)
        load_link.wait()
        products(tuple(range(PIECES)))
        for k in range(PIECES):
            if k == 2:
                pl.when(p == 6)(lambda: pl.semaphore_wait(go_sem, 1))
            send_first(k)
        for k in range(PIECES):
            send_second(k)

        @pl.when(p < 6)
        def _():
            for k in range(PIECES):
                settle(k)

        @pl.when(p == 6)
        def _():
            for k in range(PIECES):
                settle(k)
                down_step(k, True)

        @pl.when((p > 0) & (p < 6))
        def _():
            for k in range(PIECES):
                down_step(k, True)

        @pl.when(p == 0)
        def _():
            for k in range(PIECES):
                down_step(k, False)

    for k in range(PIECES):
        for c in range(2):
            pl.when(p < 7)(lambda: up("sent", k, c))
            pl.when(p > 0)(lambda: down("sent", k, c))
        for copy in phase1(k)[1] + phase2(k)[1]:
            copy.wait_send()


def local(rhs, diag, back, back_near, fore, fore_near, link, donor, dest, slot):
    links = link.shape[1]
    piece = (PIECES, 2, ROWS, 640)
    near = pltpu.VMEM((6, ROWS, 640), BF)
    each = pltpu.SemaphoreType.DMA((PIECES, 2, 3))
    sems = pltpu.SemaphoreType.DMA((PIECES, 3))
    anywhere = pl.BlockSpec(memory_space=pl.ANY)
    scalars = pl.BlockSpec(memory_space=pltpu.SMEM)
    return pl.pallas_call(
        kernel,
        out_shape=pltpu.VMEM(rhs.shape, BF),
        in_specs=[anywhere] * 5 + [scalars] * 5,
        out_specs=pl.BlockSpec(memory_space=pltpu.VMEM),
        scratch_shapes=[
            pltpu.VMEM(rhs.shape[1:], F32),
            pltpu.VMEM(diag.shape[1:], BF),
            pltpu.VMEM(back.shape[1:], BF),
            pltpu.VMEM(fore.shape[1:], BF),
            pltpu.VMEM(link.shape[1:], BF),
            pltpu.VMEM(back.shape[1:], BF),
            pltpu.VMEM(piece, F32),
            pltpu.VMEM(piece, BF),
            pltpu.VMEM(piece, BF),
            pltpu.VMEM((PIECES, links + 1, ROWS, 640), BF),
            pltpu.VMEM((PIECES, 4, 4, 2, ROWS, 640), BF),
            pltpu.VMEM((PIECES, 4, 2, ROWS, 640), BF),
            pltpu.VMEM((PIECES, 3, 4, 2, ROWS, 640), BF),
            pltpu.VMEM((PIECES, 3, 2, ROWS, 640), BF),
            pltpu.SMEM((2, 32), jnp.int32),
        ]
        + [near] * (2 * PIECES)
        + [pltpu.SemaphoreType.DMA((5,))]
        + [each] * 4
        + [sems] * 4
        + [pltpu.SemaphoreType.REGULAR],
        compiler_params=pltpu.CompilerParams(
            collective_id=0, has_side_effects=True, vmem_limit_bytes=58 * 1024 * 1024
        ),
        cost_estimate=pl.CostEstimate(
            flops=2 * 32 * 640 * 640 * 640, bytes_accessed=20_000_000, transcendentals=0
        ),
    )(rhs, diag, back, fore, link, back_near, fore_near, donor, dest[:, :, 0], slot)


def solution(mesh):
    return jax.shard_map(
        local,
        mesh=mesh,
        in_specs=(
            P("plane", "dom", None, None),
            P("plane", "dom", None, None),
            P("plane", "dom", None, None, None),
            P("plane", "dom", None),
            P("plane", "dom", None, None, None),
            P("plane", "dom", None),
            P("plane", "dom", None, None),
            P("plane", "dom"),
            P("plane", "dom", None),
            P("plane", "dom"),
        ),
        out_specs=P("plane", "dom", None, None),
        check_vma=False,
    )
```

```python
import functools

import jax
import jax.numpy as jnp
from jax import lax
from jax.experimental import pallas as pl
from jax.experimental.pallas import tpu as pltpu
from jax.sharding import PartitionSpec as P

BF, F32 = jnp.bfloat16, jnp.float32
MESH = pl.DeviceIdType.MESH
PIECES = 4
ROWS = 16


def dot(a, b):
    return jnp.dot(a, b, preferred_element_type=F32)


def kernel(
    rhs_h, diag_h, back_h, fore_h, link_h, back_near, fore_near, donor, dest, slot,
    out,
    rhs, diag, back, fore, link, coup, base, w, xs, prod, pack, part, first, second,
    pick,
    near_u0, near_u1, near_u2, near_u3, near_d0, near_d1, near_d2, near_d3,
    load_sem, up_s, up_r, dn_s, dn_r, f1_s, f1_r, f2_s, f2_r, go_sem,
):
    p, d = lax.axis_index("plane"), lax.axis_index("dom")
    x, y = d // 4, d % 4
    near_u = (near_u0, near_u1, near_u2, near_u3)
    near_d = (near_d0, near_d1, near_d2, near_d3)
    links = link.shape[0]

    loads = [
        pltpu.make_async_copy(h.at[0], v, load_sem.at[i])
        for i, (h, v) in enumerate(
            ((rhs_h, rhs), (diag_h, diag), (back_h, back), (link_h, link), (fore_h, fore))
        )
    ]
    load_rhs, load_diag, load_back, load_link, load_fore = loads
    load_diag.start()

    @pl.when(p > 0)
    def _():
        load_back.start()

    load_rhs.start()

    barrier = pltpu.get_barrier_semaphore()

    def greet(plane, dom):
        pl.semaphore_signal(
            barrier, inc=1, device_id={"plane": plane, "dom": dom}, device_id_type=MESH
        )

    for step in (-1, 1):
        @pl.when((p + step >= 0) & (p + step < 8))
        def _():
            greet(p + step, d)

            @pl.when(d > 0)
            def _():
                greet(p + step, d - 1)

            @pl.when(d < 15)
            def _():
                greet(p + step, d + 1)

    for j in (1, 2, 3):
        greet(p, x * 4 + (y + j) % 4)
        greet(p, ((x + j) % 4) * 4 + y)
    beside = jnp.where((d > 0) & (d < 15), 3, 2)
    planes = jnp.where((p > 0) & (p < 7), 2, 1)

    def move(act, k, c, step, src, near, ss, rs):
        def one(n, shift):
            return pltpu.make_async_remote_copy(
                src_ref=src.at[k, c],
                dst_ref=near[k].at[2 - 2 * shift + c],
                send_sem=ss.at[k, c, n],
                recv_sem=rs.at[k, c, n],
                device_id={"plane": p + step, "dom": d + shift},
                device_id_type=MESH,
            )

        right, left, same = one(0, 1), one(1, -1), one(2, 0)
        if act == "recv":
            pl.when(d > 0)(right.wait_recv)
            pl.when(d < 15)(left.wait_recv)
            same.wait_recv()
        else:
            do = (lambda m: m.start()) if act == "start" else (lambda m: m.wait_send())
            do(same)
            pl.when(d < 15)(lambda: do(right))
            pl.when(d > 0)(lambda: do(left))

    up = functools.partial(move, step=1, src=w, near=near_u, ss=up_s, rs=up_r)
    down = functools.partial(move, step=-1, src=xs, near=near_d, ss=dn_s, rs=dn_r)

    def spot(table, c, s):
        start = (d - 1) * 2
        return jnp.clip(start + table[0, c, s], 0, 31) - start

    def compose(src, dst):
        def body(i, _):
            dst[i // 2, i % 2] = dot(src[i // 2, i % 2], diag[i // 2]).astype(BF)
            return 0

        lax.fori_loop(0, 4, body, 0)

    load_diag.wait()

    @pl.when(p > 0)
    def _():
        load_back.wait()
        compose(back, coup)

    load_rhs.wait()
    for c in range(2):
        whole = dot(rhs[c].astype(BF), diag[c])
        for k in range(PIECES):
            base[k, c] = whole[k * ROWS:(k + 1) * ROWS]

    pl.semaphore_wait(barrier, beside * planes + 6)

    @pl.when(p == 0)
    def _():
        for k in range(PIECES):
            for c in range(2):
                w[k, c] = base[k, c].astype(BF)
                up("start", k, c)

    load_link.start()
    load_fore.start()

    def choose(i, _):
        one, two = jnp.int32(links), jnp.int32(links)
        for l in range(links):
            hit = dest[0, l] * 2 + slot[0, l] == i
            two = jnp.where(hit & (one < links), l, two)
            one = jnp.where(hit & (one == links), l, one)
        pick[0, i] = one
        pick[1, i] = two
        return 0

    def ready():
        lax.fori_loop(0, 32, choose, 0)
        for k in range(PIECES):
            prod[k, links] = jnp.zeros((ROWS, 640), BF)
        load_fore.wait()
        pl.when(p < 7)(lambda: compose(fore, back))

    pl.when((p == 3) | (p > 4))(ready)

    def up_step(k, send=False):
        for c in range(2):
            up("recv", k, c)
        for c in range(2):
            total = base[k, c]
            for s in range(2):
                total = total - dot(near_u[k][spot(back_near, c, s)], coup[c, s])
            w[k, c] = total.astype(BF)
            if send:
                up("start", k, c)

    def products(ks):
        def body(l, _):
            rows = jnp.concatenate([w[k, donor[0, l]] for k in ks], axis=0)
            got = dot(rows, link[l]).astype(BF)
            for i, k in enumerate(ks):
                prod[k, l] = got[i * ROWS:(i + 1) * ROWS]
            return 0

        lax.fori_loop(0, links, body, 0, unroll=12)

    def phase1(k):
        a = y if k % 2 == 0 else x
        found = []
        for j in (1, 2, 3):
            there = (a + j) % 4
            target = x * 4 + there if k % 2 == 0 else there * 4 + y
            found.append(pltpu.make_async_remote_copy(
                src_ref=pack.at[k, there],
                dst_ref=first.at[k, j - 1],
                send_sem=f1_s.at[k, j - 1],
                recv_sem=f1_r.at[k, j - 1],
                device_id={"plane": p, "dom": target},
                device_id_type=MESH,
            ))
        return a, found

    def phase2(k):
        b = x if k % 2 == 0 else y
        found = []
        for j in (1, 2, 3):
            there = (b + j) % 4
            target = there * 4 + y if k % 2 == 0 else x * 4 + there
            found.append(pltpu.make_async_remote_copy(
                src_ref=part.at[k, there],
                dst_ref=second.at[k, j - 1],
                send_sem=f2_s.at[k, j - 1],
                recv_sem=f2_r.at[k, j - 1],
                device_id={"plane": p, "dom": target},
                device_id_type=MESH,
            ))
        return b, found

    def send_first(k):
        for i in range(32):
            a, b, c = i // 8, (i // 2) % 4, i % 2
            cell = (b * 4 + a) * 2 + c if k % 2 == 0 else i
            pack[k, a, b, c] = prod[k, pick[0, cell]] + prod[k, pick[1, cell]]
        one, two, three = phase1(k)[1]
        for copy in (one, three, two):
            copy.start()

    def send_second(k):
        a, copies = phase1(k)
        for copy in copies:
            copy.wait_recv()

        for b in range(4):
            for c in range(2):
                total = pack[k, a, b, c].astype(F32)
                for j in range(3):
                    total = total + first[k, j, b, c].astype(F32)
                part[k, b, c] = total.astype(BF)
        one, two, three = phase2(k)[1]
        for copy in (one, three, two):
            copy.start()

    def settle(k):
        b, copies = phase2(k)
        for copy in copies:
            copy.wait_recv()
        for c in range(2):
            total = part[k, b, c].astype(F32)
            for j in range(3):
                total = total + second[k, j, c].astype(F32)
            base[k, c] = w[k, c].astype(F32) - dot(total.astype(BF), diag[c])

    def finish(k, c, value):
        value = value.astype(BF)
        xs[k, c] = value
        out[0, c, k * ROWS:(k + 1) * ROWS] = value

    def turn(k):
        for c in range(2):
            finish(k, c, base[k, c])
            down("start", k, c)

    def down_step(k, send):
        for c in range(2):
            down("recv", k, c)
        for c in range(2):
            total = base[k, c]
            for s in range(2):
                total = total - dot(near_d[k][spot(fore_near, c, s)], back[c, s])
            finish(k, c, total)
            if send:
                down("start", k, c)

    @pl.when(p == 7)
    def _():
        load_link.wait()
        for k in (0, 2):
            up_step(k)
            up_step(k + 1)
            products((k, k + 1))
            send_first(k)
            send_first(k + 1)
        send_second(0)
        send_second(1)
        pl.semaphore_signal(
            go_sem, inc=1, device_id={"plane": p - 1, "dom": d}, device_id_type=MESH
        )
        for k in range(PIECES):
            settle(k)
            turn(k)
            if k < 2:
                send_second(k + 2)

    @pl.when(p < 7)
    def _():
        @pl.when(p > 0)
        def _():
            for k in range(PIECES):
                up_step(k, True)

        pl.when((p < 3) | (p == 4))(ready)
        load_link.wait()
        products(tuple(range(PIECES)))
        for k in range(PIECES):
            if k == 2:
                pl.when(p == 6)(lambda: pl.semaphore_wait(go_sem, 1))
            send_first(k)
        for k in range(PIECES):
            send_second(k)

        @pl.when(p < 6)
        def _():
            for k in range(PIECES):
                settle(k)

        @pl.when(p == 6)
        def _():
            for k in range(PIECES):
                settle(k)
                down_step(k, True)

        @pl.when((p > 0) & (p < 6))
        def _():
            for k in range(PIECES):
                down_step(k, True)

        @pl.when(p == 0)
        def _():
            for k in range(PIECES):
                down_step(k, False)

    for k in range(PIECES):
        for c in range(2):
            pl.when(p < 7)(lambda: up("sent", k, c))
            pl.when(p > 0)(lambda: down("sent", k, c))
        for copy in phase1(k)[1] + phase2(k)[1]:
            copy.wait_send()


def local(rhs, diag, back, back_near, fore, fore_near, link, donor, dest, slot):
    links = link.shape[1]
    piece = (PIECES, 2, ROWS, 640)
    near = pltpu.VMEM((6, ROWS, 640), BF)
    each = pltpu.SemaphoreType.DMA((PIECES, 2, 3))
    sems = pltpu.SemaphoreType.DMA((PIECES, 3))
    anywhere = pl.BlockSpec(memory_space=pl.ANY)
    scalars = pl.BlockSpec(memory_space=pltpu.SMEM)
    return pl.pallas_call(
        kernel,
        out_shape=pltpu.VMEM(rhs.shape, BF),
        in_specs=[anywhere] * 5 + [scalars] * 5,
        out_specs=pl.BlockSpec(memory_space=pltpu.VMEM),
        scratch_shapes=[
            pltpu.VMEM(rhs.shape[1:], F32),
            pltpu.VMEM(diag.shape[1:], BF),
            pltpu.VMEM(back.shape[1:], BF),
            pltpu.VMEM(fore.shape[1:], BF),
            pltpu.VMEM(link.shape[1:], BF),
            pltpu.VMEM(back.shape[1:], BF),
            pltpu.VMEM(piece, F32),
            pltpu.VMEM(piece, BF),
            pltpu.VMEM(piece, BF),
            pltpu.VMEM((PIECES, links + 1, ROWS, 640), BF),
            pltpu.VMEM((PIECES, 4, 4, 2, ROWS, 640), BF),
            pltpu.VMEM((PIECES, 4, 2, ROWS, 640), BF),
            pltpu.VMEM((PIECES, 3, 4, 2, ROWS, 640), BF),
            pltpu.VMEM((PIECES, 3, 2, ROWS, 640), BF),
            pltpu.SMEM((2, 32), jnp.int32),
        ]
        + [near] * (2 * PIECES)
        + [pltpu.SemaphoreType.DMA((5,))]
        + [each] * 4
        + [sems] * 4
        + [pltpu.SemaphoreType.REGULAR],
        compiler_params=pltpu.CompilerParams(
            collective_id=0, has_side_effects=True, vmem_limit_bytes=58 * 1024 * 1024
        ),
        cost_estimate=pl.CostEstimate(
            flops=2 * 32 * 640 * 640 * 640, bytes_accessed=20_000_000, transcendentals=0
        ),
    )(rhs, diag, back, fore, link, back_near, fore_near, donor, dest[:, :, 0], slot)


def solution(mesh):
    return jax.shard_map(
        local,
        mesh=mesh,
        in_specs=(
            P("plane", "dom", None, None),
            P("plane", "dom", None, None),
            P("plane", "dom", None, None, None),
            P("plane", "dom", None),
            P("plane", "dom", None, None, None),
            P("plane", "dom", None),
            P("plane", "dom", None, None),
            P("plane", "dom"),
            P("plane", "dom", None),
            P("plane", "dom"),
        ),
        out_specs=P("plane", "dom", None, None),
        check_vma=False,
    )
```
